256 devices in a mesh: batch: 16 (over z, core), tensor: 16 (over x, y).
Axes of the slice: x: 4, y: 4, z: 8, core: 2. Of those that a mesh axis runs over, the one named last changes fastest.
Arguments:
- tokens_qkv: bfloat16 [256, 2, 3, 4096], P('batch', None, None, 'tensor'), may hold values from -6 to 6
- residual_in: bfloat16 [256, 2, 8192], P('batch', None, 'tensor'), may hold values from -6 to 6
- state: float32 [256, 32, 128, 128], P('batch', 'tensor'), may hold values from -6 to 6
- decay_table: float32 [16], replicated, may hold values from 0.3 to 0.999
- decay_index: int32 [32], P('tensor'), may hold values from 0 to 15
- active: int32 [256], P('batch'), may hold values 0 or 1
- move_slot: int32 [16, 16], P('batch'), may hold values from 0 to 15, as said below
- move_dest: int32 [16, 16], P('batch'), may hold values from 0 to 15, as said below
- norm_gain: bfloat16 [8192], P('tensor'), may hold values from 0.5 to 1.5
- out_weight: bfloat16 [4096, 8192], P('tensor'), may hold values from -0.09375 to 0.09375
Outputs:
- normed: bfloat16 [256, 2, 8192], P('batch', None, 'tensor')
- residual_out: bfloat16 [256, 2, 8192], P('batch', None, 'tensor')
- new_state: float32 [256, 32, 128, 128], P('batch', 'tensor')
- arrived: float32 [512, 32, 128, 128], P('batch', 'tensor')
The draws below stay inside these ranges and needn't reach their ends.
Inputs may be any that keep to these rules, and one draw needn't show every extreme that they name: `move_slot`: in each group's list the slots are distinct. `move_dest`: an entry naming its own group moves nothing; at most 2 entries of one list name one other group, and in every list some other group is named by exactly 2 entries.
All inputs are finite; a program needn't handle non-finite values. No bound on the sum of `active` on one device may be relied on, other than what follows from the above.
Results may differ from the reference program's by a relative error of at most 0.004.
Values may be sent and summed in bfloat16 or wider, within the bound.
No kernel may reach another device: no remote copies, remote signals or barrier semaphores. Data moves between devices by JAX's collectives and lax.ppermute only.
A program may use at most 64 MiB of HBM per device.

```python
import math
import jax
import jax.numpy as jnp
from jax import lax

D = 8192
HEADS = 32
HEAD_DIM = 128
STEPS = 2
TABLE = 16
CAP = 2
REQ_DEV = 16
MOVE = 16
REQS = 256
N_BATCH = 16


def move_lists(key):
    keys = jax.random.split(key, N_BATCH)

    def one_group(group_key, group):
        slot_key, offset_key, stay_key, full_key = jax.random.split(group_key, 4)
        slots = jax.random.permutation(slot_key, REQ_DEV)[:MOVE]
        offsets = jax.random.permutation(offset_key, N_BATCH - 1)[:MOVE // CAP] + 1
        block_dest = (group + offsets) % N_BATCH
        dests = jnp.repeat(block_dest, CAP)
        stays = jnp.where(jax.random.randint(stay_key, (MOVE,), 0, 4) == 0, 1, 0)
        full_block = jax.random.randint(full_key, (), 0, MOVE // CAP)
        stays = jnp.where(jnp.arange(MOVE) // CAP == full_block, 0, stays)
        dests = jnp.where(stays > 0, group, dests)
        return (slots.astype(jnp.int32), dests.astype(jnp.int32))
    return jax.vmap(one_group)(keys, jnp.arange(N_BATCH))


def draw_move_slot(key, part):
    slots, dests = move_lists(key)
    return slots


def draw_move_dest(key, part):
    slots, dests = move_lists(key)
    return dests


def set_ends(values, stream_key, low, high):
    index_at = [jax.random.randint(jax.random.fold_in(stream_key, axis), (), 0, length) for axis, length in enumerate(values.shape)]
    longest = values.shape.index(max(values.shape))
    next_to = index_at[:longest] + [(index_at[longest] + 1) % values.shape[longest]] + index_at[longest + 1:]
    return values.at[tuple(index_at)].set(low).at[tuple(next_to)].set(high)


def block_levels(key, dims, cuts, least, high):
    gain = 1.0
    for axis_at, blocks in cuts:
        draws = jax.random.uniform(jax.random.fold_in(jax.random.fold_in(key, 6), axis_at), (blocks,), jnp.float32, least / len(cuts), high / len(cuts))
        gain = gain * jnp.repeat(jnp.exp(draws), dims[axis_at] // blocks).reshape((-1,) + (1,) * (len(dims) - 1 - axis_at))
    return gain


def noise(key, extent, spread, reach, shards=(), dtype=jnp.bfloat16):
    entries = jax.random.normal(key, extent, jnp.float32) * spread
    if len(shards) > 0:
        entries = block_levels(key, extent, shards, -0.22, 0.18) * entries
    return jnp.clip(entries, min=-reach, max=reach).astype(dtype)


def setup_inputs(seed: int = 0) -> dict:
    key_list = jax.random.split(jax.random.key(seed), 11)
    tokens_qkv = noise(key_list[0], (REQS, STEPS, 3, HEADS * HEAD_DIM), 1.0, 6.0, ((0, 16), (3, 16)))
    residual_in = noise(key_list[1], (REQS, STEPS, D), 1.0, 6.0, ((0, 16), (2, 16)))
    state = noise(key_list[2], (REQS, HEADS, HEAD_DIM, HEAD_DIM), 1.0, 6.0, ((0, 16), (1, 16)), jnp.float32)
    decay_table = jnp.clip(jnp.exp(jax.random.uniform(key_list[3], (TABLE,), jnp.float32, math.log(0.3), math.log(0.999))), 0.3, 0.999)
    decay_index = set_ends(jax.random.randint(key_list[4], (HEADS,), 0, TABLE), jax.random.fold_in(key_list[4], 1), 0, TABLE - 1).astype(jnp.int32)
    active = set_ends((jax.random.randint(key_list[5], (REQS,), 0, 4) < 3).astype(jnp.int32), jax.random.fold_in(key_list[5], 1), 0, 1)
    move_slot = draw_move_slot(jax.random.fold_in(key_list[10], 71), 0)
    move_dest = draw_move_dest(jax.random.fold_in(key_list[10], 71), 0)
    norm_gain = jnp.clip(1.0 + 0.1 * jax.random.normal(key_list[8], (D,), jnp.float32), 0.5, 1.5).astype(jnp.bfloat16)
    out_weight = noise(key_list[9], (HEADS * HEAD_DIM, D), (HEADS * HEAD_DIM) ** -0.5, 0.09375, ((0, 16),))
    return dict(tokens_qkv=tokens_qkv, residual_in=residual_in, state=state, decay_table=decay_table, decay_index=decay_index, active=active, move_slot=move_slot, move_dest=move_dest, norm_gain=norm_gain, out_weight=out_weight)


def head_decays(decay_table, decay_index):
    table_ids = jnp.arange(decay_table.shape[0]).astype(jnp.int32)
    picked = jnp.where(decay_index[:, None] == table_ids[None, :], decay_table[None, :], 0.0)
    return lax.optimization_barrier(jnp.sum(picked, axis=1))

def advance(current, keys, values, flags, gamma):
    updated = gamma[None, :, None, None] * current + keys[..., :, None] * values[..., None, :]
    return jnp.where(flags[:, None, None, None], updated, current)

def readout(current, query, flags):
    raw = jnp.einsum('rhi,rhij->rhj', query, current, precision=lax.Precision.HIGHEST)
    scaled = raw * lax.rsqrt(lax.optimization_barrier(jnp.mean(raw * raw, axis=-1, keepdims=True)) + 1e-06)
    return jnp.where(flags[:, None, None], scaled, 0.0)

def run_group(tokens, current, flags, gamma):
    count = current.shape[0]
    heads = current.shape[1]
    width = current.shape[2]
    outputs = []
    for step in range(STEPS):
        parts = tokens[:, step].astype(jnp.float32).reshape(count, 3, heads, width)
        current = advance(current, parts[:, 1], parts[:, 2], flags, gamma)
        outputs.append(readout(current, parts[:, 0], flags).reshape(count, heads * width))
    return (current, jnp.stack(outputs, axis=1).astype(jnp.bfloat16))

def entry_ranks(dests):
    count = dests.shape[-1]
    order = jnp.arange(count)
    same = dests[..., :, None] == dests[..., None, :]
    earlier = order[None, :] < order[:, None]
    return lax.optimization_barrier(jnp.sum(jnp.where(same & earlier, 1, 0), axis=-1)).astype(jnp.int32)

def reference(tokens_qkv, residual_in, state, decay_table, decay_index, active, move_slot, move_dest, norm_gain, out_weight):
    gamma = head_decays(decay_table, decay_index)
    groups = move_slot.shape[0]
    tokens_grouped = tokens_qkv.reshape((groups, REQ_DEV) + tokens_qkv.shape[1:])
    state_grouped = state.reshape((groups, REQ_DEV) + state.shape[1:])
    flags_grouped = (active > 0).reshape(groups, REQ_DEV)
    final, heads_out = lax.map(lambda item: run_group(item[0], item[1], item[2], gamma), (tokens_grouped, state_grouped, flags_grouped))
    heads_out = heads_out.reshape(REQS * STEPS, HEADS * HEAD_DIM)
    proj = jnp.dot(heads_out, out_weight, preferred_element_type=jnp.float32).reshape(REQS, STEPS, D)
    hsum = residual_in.astype(jnp.float32) + proj
    normed = hsum * lax.rsqrt(lax.optimization_barrier(jnp.mean(hsum * hsum, axis=-1, keepdims=True)) + 1e-05) * norm_gain.astype(jnp.float32)
    group_ids = jnp.arange(groups).astype(jnp.int32)
    moving = move_dest != group_ids[:, None]
    slot_ids = jnp.arange(REQ_DEV).astype(jnp.int32)
    departed = jnp.any(moving[:, :, None] & (move_slot[:, :, None] == slot_ids[None, None, :]), axis=1)
    new_state = jnp.where(departed[:, :, None, None, None], 0.0, final).reshape(state.shape)
    ranks = entry_ranks(move_dest)
    positions = jnp.arange(CAP).astype(jnp.int32)

    def to_dest(dest):
        match = (moving & (move_dest == dest))[:, None, :] & (ranks[:, None, :] == positions[None, :, None])
        chosen = lax.optimization_barrier(jnp.sum(jnp.where(match, move_slot[:, None, :], 0), axis=2)).astype(jnp.int32)
        valid = jnp.any(match, axis=2)
        rows = final[group_ids[:, None], chosen]
        return jnp.where(valid[:, :, None, None, None], rows, 0.0).reshape((groups * CAP,) + final.shape[2:])
    arrived = lax.map(to_dest, group_ids).reshape((groups * groups * CAP,) + final.shape[2:])
    return (normed.astype(jnp.bfloat16), hsum.astype(jnp.bfloat16), new_state, arrived)
```

```python
import functools

import jax
import jax.numpy as jnp
from jax import lax
from jax.experimental import pallas as pl
from jax.experimental.pallas import tpu as pltpu
from jax.sharding import PartitionSpec as P

D = 8192
STEPS = 2
CAP = 2
SIDE = 4
W = 128

SMEM = pl.BlockSpec(memory_space=pltpu.SMEM)
VMEM = pl.BlockSpec(memory_space=pltpu.VMEM)


def decay(table_ref, index_ref, h):
    return table_ref[index_ref[h]]


def rows_of(k, v, gamma, h):
    kh = k[:, h * W : (h + 1) * W]
    vh = v[:, h * W : (h + 1) * W]
    row = lax.broadcasted_iota(jnp.int32, (8, W), 0)
    first = gamma * kh[0:1]
    hi = first.astype(jnp.bfloat16).astype(jnp.float32)
    mid = (first - hi).astype(jnp.bfloat16).astype(jnp.float32)
    low = first - hi - mid
    left = jnp.where(row == 0, hi, jnp.where(row == 1, mid, jnp.where(row == 2, low, jnp.where(row == 3, kh[1:2], 0.0))))
    right = jnp.where(row < 3, vh[0:1], jnp.where(row == 3, vh[1:2], 0.0))
    return left, right


def outer(left, right):
    return lax.dot_general(
        left.astype(jnp.bfloat16),
        right.astype(jnp.bfloat16),
        (((0,), (0,)), ((), ())),
        preferred_element_type=jnp.float32,
    )


def leave_kernel(table_ref, index_ref, active_ref, slot_ref, dest_ref, tok_ref, state_ref, out_ref, count_ref):
    me = lax.axis_index("batch")
    entries = slot_ref.shape[1]
    heads = state_ref.shape[1]
    for g in range(count_ref.shape[0]):
        count_ref[g] = 0
    out_ref[...] = jnp.zeros_like(out_ref)

    def entry(j, carry):
        slot = slot_ref[0, j]
        dest = dest_ref[0, j]
        position = count_ref[dest]
        count_ref[dest] = position + 1

        @pl.when((dest != me) & (position < CAP))
        def _():
            on = active_ref[slot] > 0
            tokens = tok_ref[slot].astype(jnp.float32)
            for h in range(heads):
                gamma = decay(table_ref, index_ref, h)
                left, right = rows_of(tokens[1], tokens[2], gamma, h)
                left = jnp.where(on, left, 0.0)
                keep = jnp.where(on, gamma * gamma, 1.0)
                final = keep * state_ref[slot, h] + outer(left, right)
                out_ref[dest * CAP + position, h] = final.astype(jnp.bfloat16)

        return carry

    lax.fori_loop(0, entries, entry, 0)


def decode_kernel(
    table_ref, index_ref, active_ref, slot_ref, dest_ref, tok_ref, state_ref, new_ref, heads_ref, gone_ref
):
    me = lax.axis_index("batch")
    entries = slot_ref.shape[1]
    heads = state_ref.shape[1]
    i = pl.program_id(0)

    @pl.when(i == 0)
    def _():
        for s in range(gone_ref.shape[0]):
            gone_ref[s] = 0
        for j in range(entries):
            slot = slot_ref[0, j]
            moves = jnp.where(dest_ref[0, j] != me, 1, 0)
            gone_ref[slot] = gone_ref[slot] + moves

    on = active_ref[i] > 0
    gone = gone_ref[i] > 0
    tokens = tok_ref[0].astype(jnp.float32)
    query, key, value = tokens[0], tokens[1], tokens[2]
    row = lax.broadcasted_iota(jnp.int32, (8, W), 0)
    wide = lax.broadcasted_iota(jnp.int32, (8, 2 * W), 0)
    lane = lax.broadcasted_iota(jnp.int32, (8, 2 * W), 1)
    ones = jnp.where((wide == 4) & (lane < W), 1.0, jnp.where((wide == 5) & (lane >= W), 1.0, 0.0))
    for h in range(heads):
        part = slice(h * W, (h + 1) * W)
        q, k, v = query[:, part], key[:, part], value[:, part]
        gamma = decay(table_ref, index_ref, h)
        left, right = rows_of(key, value, gamma, h)
        left = jnp.where(row == 4, q[0:1], jnp.where(row == 5, q[1:2], left))
        mixed = outer(left, jnp.concatenate([right, ones], axis=1))
        before = state_ref[0, h]
        raw1 = gamma * jnp.sum(mixed[:, W : 2 * W] * before, axis=0, keepdims=True)
        raw1 = raw1 + jnp.sum(q[0:1] * k[0:1], axis=1, keepdims=True) * v[0:1]
        final = (gamma * gamma) * before + mixed[:, :W]
        raw2 = jnp.sum(mixed[:, 2 * W :] * final, axis=0, keepdims=True)
        raw = jnp.where(row == 0, raw1, jnp.where(row == 1, raw2, 0.0))
        scaled = raw * lax.rsqrt(jnp.mean(raw * raw, axis=1, keepdims=True) + 1e-06)
        heads_ref[0, :, part] = jnp.where(on, scaled, 0.0)
        final = jnp.where(on, final, before)
        new_ref[0, h] = jnp.where(gone, 0.0, final)


def project_kernel(heads_ref, weight_ref, *out_refs):
    me = lax.axis_index("tensor")
    x = me // SIDE
    y = me % SIDE
    share = weight_ref.shape[1] // (SIDE * SIDE)
    count, padded, depth = heads_ref.shape
    rows = count * STEPS
    row = lax.broadcasted_iota(jnp.int32, (rows, count * padded), 0)
    source = lax.broadcasted_iota(jnp.int32, (rows, count * padded), 1)
    pick = jnp.where(source == (row // STEPS) * padded + row % STEPS, 1.0, 0.0).astype(jnp.bfloat16)
    heads = heads_ref[...].reshape(count * padded, depth).astype(jnp.bfloat16)
    heads = jnp.dot(pick, heads, preferred_element_type=jnp.float32).astype(jnp.bfloat16)
    for dx in range(SIDE):
        for dy in range(SIDE):
            block = ((x + dx) % SIDE) * SIDE + (y + dy) % SIDE
            columns = pl.ds(pl.multiple_of(block * share, share), share)
            out_refs[dx][dy] = jnp.dot(heads, weight_ref[:, columns], preferred_element_type=jnp.float32)


def add_kernel(a_ref, b_ref, c_ref, d_ref, *out_refs):
    for dy in range(SIDE):
        out_refs[dy][...] = (a_ref[dy] + b_ref[dy]) + (c_ref[dy] + d_ref[dy])


def residual_kernel(residual_ref, a_ref, b_ref, c_ref, d_ref, hsum_ref, square_ref):
    hsum = residual_ref[...].astype(jnp.float32) + ((a_ref[...] + b_ref[...]) + (c_ref[...] + d_ref[...]))
    hsum_ref[...] = hsum
    square_ref[...] = jnp.broadcast_to(jnp.sum(hsum * hsum, axis=1, keepdims=True), square_ref.shape)


def shift_x(value, d):
    return lax.ppermute(
        value, "tensor", [(x * SIDE + y, ((x + d) % SIDE) * SIDE + y) for x in range(SIDE) for y in range(SIDE)]
    )


def shift_y(value, d):
    return lax.ppermute(
        value, "tensor", [(x * SIDE + y, x * SIDE + (y + d) % SIDE) for x in range(SIDE) for y in range(SIDE)]
    )


def body(
    tokens_qkv,
    residual_in,
    state,
    decay_table,
    decay_index,
    active,
    move_slot,
    move_dest,
    norm_gain,
    out_weight,
):
    count, heads, width, _ = state.shape
    groups = lax.axis_size("batch")
    rows = count * STEPS
    share = residual_in.shape[2]
    f32 = jnp.float32
    tokens = jnp.transpose(tokens_qkv, (0, 2, 1, 3))
    scalars = (decay_table, decay_index, active, move_slot, move_dest)

    leaving = pl.pallas_call(
        leave_kernel,
        out_shape=jax.ShapeDtypeStruct((groups * CAP, heads, width, width), jnp.bfloat16),
        in_specs=[SMEM] * 5 + [VMEM] * 2,
        out_specs=VMEM,
        scratch_shapes=[pltpu.SMEM((groups,), jnp.int32)],
        compiler_params=pltpu.CompilerParams(vmem_limit_bytes=24 << 20),
        cost_estimate=pl.CostEstimate(flops=32 * 10 * width * width, bytes_accessed=4 << 20, transcendentals=0),
        name="leave",
    )(*scalars, tokens, state)
    landed = lax.all_to_all(leaving, "batch", split_axis=0, concat_axis=0, tiled=True)

    new_state, heads_out = pl.pallas_call(
        decode_kernel,
        grid=(count,),
        out_shape=(
            jax.ShapeDtypeStruct(state.shape, f32),
            jax.ShapeDtypeStruct((count, 8, heads * width), f32),
        ),
        in_specs=[SMEM] * 5
        + [
            pl.BlockSpec((1, 3, STEPS, heads * width), lambda i: (i, 0, 0, 0)),
            pl.BlockSpec((1, heads, width, width), lambda i: (i, 0, 0, 0)),
        ],
        out_specs=(
            pl.BlockSpec((1, heads, width, width), lambda i: (i, 0, 0, 0)),
            pl.BlockSpec((1, 8, heads * width), lambda i: (i, 0, 0)),
        ),
        scratch_shapes=[pltpu.SMEM((count,), jnp.int32)],
        compiler_params=pltpu.CompilerParams(vmem_limit_bytes=24 << 20),
        cost_estimate=pl.CostEstimate(flops=32 * 20 * width * width, bytes_accessed=4 << 20, transcendentals=0),
        name="decode",
    )(*scalars, tokens, state)

    parts = pl.pallas_call(
        project_kernel,
        out_shape=[jax.ShapeDtypeStruct((SIDE, rows, share), f32)] * SIDE,
        in_specs=[VMEM] * 2,
        out_specs=[VMEM] * SIDE,
        compiler_params=pltpu.CompilerParams(vmem_limit_bytes=24 << 20),
        cost_estimate=pl.CostEstimate(flops=2 * rows * heads * width * D, bytes_accessed=5 << 20, transcendentals=0),
        name="project",
    )(heads_out, out_weight)
    lines = [parts[0]] + [shift_x(parts[d], d) for d in range(1, SIDE)]
    sums = pl.pallas_call(
        add_kernel,
        out_shape=[jax.ShapeDtypeStruct((rows, share), f32)] * SIDE,
        in_specs=[VMEM] * SIDE,
        out_specs=[VMEM] * SIDE,
        name="add",
    )(*lines)
    terms = [sums[0]] + [shift_y(sums[d], d) for d in range(1, SIDE)]
    residual = residual_in.reshape(rows, share)
    hsum, square = pl.pallas_call(
        residual_kernel,
        out_shape=(jax.ShapeDtypeStruct((rows, share), f32), jax.ShapeDtypeStruct((rows, W), f32)),
        in_specs=[VMEM] * 5,
        out_specs=(VMEM, VMEM),
        name="residual",
    )(residual, *terms)
    square = square + (shift_x(square, 1) + shift_x(square, 2) + shift_x(square, 3))
    square = square + (shift_y(square, 1) + shift_y(square, 2) + shift_y(square, 3))
    normed = hsum * lax.rsqrt(square[:, :1] / D + 1e-05) * norm_gain.astype(f32)

    def place(value):
        return value.astype(jnp.bfloat16).reshape(count, STEPS, share)

    return (place(normed), place(hsum), new_state, landed.astype(f32))


def solution(mesh):
    return jax.shard_map(
        body,
        mesh=mesh,
        in_specs=(
            P("batch", None, None, "tensor"),
            P("batch", None, "tensor"),
            P("batch", "tensor", None, None),
            P(),
            P("tensor"),
            P("batch"),
            P("batch", None),
            P("batch", None),
            P("tensor"),
            P("tensor", None),
        ),
        out_specs=(
            P("batch", None, "tensor"),
            P("batch", None, "tensor"),
            P("batch", "tensor", None, None),
            P("batch", "tensor", None, None),
        ),
        check_vma=False,
    )
```

```python
import jax
import jax.numpy as jnp
from jax import lax
from jax.experimental import pallas as pl
from jax.experimental.pallas import tpu as pltpu
from jax.sharding import PartitionSpec as P

D = 8192
STEPS = 2
CAP = 2
SIDE = 4
W = 128

SMEM = pl.BlockSpec(memory_space=pltpu.SMEM)
VMEM = pl.BlockSpec(memory_space=pltpu.VMEM)
HBM = pl.BlockSpec(memory_space=pltpu.HBM)


def decay(table_ref, index_ref, h):
    return table_ref[index_ref[h]]


def rows_of(k, v, gamma, h):
    kh = k[:, h * W : (h + 1) * W]
    vh = v[:, h * W : (h + 1) * W]
    row = lax.broadcasted_iota(jnp.int32, (8, W), 0)
    first = gamma * kh[0:1]
    hi = first.astype(jnp.bfloat16).astype(jnp.float32)
    mid = (first - hi).astype(jnp.bfloat16).astype(jnp.float32)
    low = first - hi - mid
    left = jnp.where(row == 0, hi, jnp.where(row == 1, mid, jnp.where(row == 2, low, jnp.where(row == 3, kh[1:2], 0.0))))
    right = jnp.where(row < 3, vh[0:1], jnp.where(row == 3, vh[1:2], 0.0))
    return left, right


def outer(left, right):
    return lax.dot_general(
        left.astype(jnp.bfloat16),
        right.astype(jnp.bfloat16),
        (((0,), (0,)), ((), ())),
        preferred_element_type=jnp.float32,
    )


def leave_kernel(
    table_any,
    index_any,
    active_any,
    slot_any,
    dest_any,
    tok_any,
    state_any,
    out_any,
    table_ref,
    index_ref,
    active_ref,
    slot_ref,
    dest_ref,
    tok_ref,
    state_ref,
    buf_ref,
    map_ref,
    in_sem,
    out_sem,
):
    me = lax.axis_index("batch")
    entries = slot_ref.shape[1]
    heads = state_ref.shape[1]
    groups = map_ref.shape[0] // CAP
    pairs = (
        (state_any, state_ref),
        (tok_any, tok_ref),
        (slot_any, slot_ref),
        (dest_any, dest_ref),
        (active_any, active_ref),
        (table_any, table_ref),
        (index_any, index_ref),
    )
    loads = [pltpu.make_async_copy(a, b, in_sem.at[n]) for n, (a, b) in enumerate(pairs)]
    for load in loads:
        load.start()
    for n in range(map_ref.shape[0]):
        map_ref[n] = -1
    for load in loads[2:]:
        load.wait()

    def entry(j, carry):
        dest = dest_ref[0, j]
        base = dest * CAP
        taken = jnp.where(map_ref[base] >= 0, 1, 0)

        @pl.when(dest != me)
        def _():
            map_ref[base + taken] = slot_ref[0, j]

        return carry

    lax.fori_loop(0, entries, entry, 0)
    loads[1].wait()
    loads[0].wait()
    def store_of(n):
        part = pl.ds(n * CAP, CAP)
        return pltpu.make_async_copy(buf_ref.at[part], out_any.at[part], out_sem.at[n])

    def fill(n, carry):
        for position in range(CAP):
            found = map_ref[n * CAP + position]
            slot = jnp.maximum(found, 0)
            on = jnp.where(active_ref[slot] > 0, 1.0, 0.0)
            tokens = tok_ref[slot].astype(jnp.float32)
            for h in range(heads):
                gamma = decay(table_ref, index_ref, h)
                left, right = rows_of(tokens[1], tokens[2], gamma, h)
                keep = jnp.where(on > 0.0, gamma * gamma, 1.0)
                final = keep * state_ref[slot, h] + outer(left * on, right)
                final = jnp.where(found >= 0, final, 0.0)
                buf_ref[n * CAP + position, h] = final.astype(jnp.bfloat16)
        store_of(n).start()
        return carry

    lax.fori_loop(0, groups, fill, 0, unroll=2)
    for n in range(groups):
        store_of(n).wait()


def decode_kernel(
    table_any,
    index_any,
    active_any,
    slot_any,
    dest_any,
    tok_ref,
    state_ref,
    weight_any,
    after_any,
    new_ref,
    part0_any,
    part1_any,
    part2_any,
    part3_any,
    table_ref,
    index_ref,
    active_ref,
    slot_ref,
    dest_ref,
    gone_ref,
    heads_ref,
    weight_ref,
    parts_ref,
    scalar_sem,
    weight_sem,
    parts_sem,
):
    parts_any = (part0_any, part1_any, part2_any, part3_any)
    me = lax.axis_index("batch")
    entries = slot_ref.shape[1]
    heads = state_ref.shape[1]
    batch = state_ref.shape[0]
    i = pl.program_id(0)
    load = pltpu.make_async_copy(weight_any, weight_ref, weight_sem)

    @pl.when(i == 0)
    def _():
        pairs = (
            (table_any, table_ref),
            (index_any, index_ref),
            (active_any, active_ref),
            (slot_any, slot_ref),
            (dest_any, dest_ref),
        )
        copies = [pltpu.make_async_copy(a, b, scalar_sem.at[n]) for n, (a, b) in enumerate(pairs)]
        for copy in copies:
            copy.start()
        load.start()
        for copy in copies:
            copy.wait()
        for s in range(gone_ref.shape[0]):
            gone_ref[s] = 0
        for j in range(entries):
            slot = slot_ref[0, j]
            moves = jnp.where(dest_ref[0, j] != me, 1, 0)
            gone_ref[slot] = gone_ref[slot] + moves

    row = lax.broadcasted_iota(jnp.int32, (8, W), 0)
    wide = lax.broadcasted_iota(jnp.int32, (8, 2 * W), 0)
    lane = lax.broadcasted_iota(jnp.int32, (8, 2 * W), 1)
    ones = jnp.where((wide == 4) & (lane < W), 1.0, jnp.where((wide == 5) & (lane >= W), 1.0, 0.0))
    for b in range(batch):
        r = i * batch + b
        on = active_ref[r] > 0
        gone = gone_ref[r] > 0
        tokens = tok_ref[b].astype(jnp.float32)
        query, key, value = tokens[0], tokens[1], tokens[2]
        for h in range(heads):
            part = slice(h * W, (h + 1) * W)
            q, k, v = query[:, part], key[:, part], value[:, part]
            gamma = decay(table_ref, index_ref, h)
            left, right = rows_of(key, value, gamma, h)
            left = jnp.where(row == 4, q[0:1], jnp.where(row == 5, q[1:2], left))
            mixed = outer(left, jnp.concatenate([right, ones], axis=1))
            before = state_ref[b, h]
            raw1 = gamma * jnp.sum(mixed[:, W : 2 * W] * before, axis=0, keepdims=True)
            raw1 = raw1 + jnp.sum(q[0:1] * k[0:1], axis=1, keepdims=True) * v[0:1]
            final = (gamma * gamma) * before + mixed[:, :W]
            raw2 = jnp.sum(mixed[:, 2 * W :] * final, axis=0, keepdims=True)
            raw = jnp.where(row == 0, raw1, jnp.where(row == 1, raw2, 0.0))
            scaled = raw * lax.rsqrt(jnp.mean(raw * raw, axis=1, keepdims=True) + 1e-06)
            heads_ref[r, :, part] = jnp.where(on, scaled, 0.0)
            final = jnp.where(on, final, before)
            new_ref[b, h] = jnp.where(gone, 0.0, final)

    @pl.when(i == pl.num_programs(0) - 1)
    def _():
        count, padded, depth = heads_ref.shape
        rows = count * STEPS
        line = lax.broadcasted_iota(jnp.int32, (rows, count * padded), 0)
        source = lax.broadcasted_iota(jnp.int32, (rows, count * padded), 1)
        pick = jnp.where(source == (line // STEPS) * padded + line % STEPS, 1.0, 0.0).astype(jnp.bfloat16)
        out = heads_ref[...].reshape(count * padded, depth).astype(jnp.bfloat16)
        out = jnp.dot(pick, out, preferred_element_type=jnp.float32).astype(jnp.bfloat16)
        load.wait()
        share = parts_ref.shape[3]
        column = lax.axis_index("tensor")
        stores = []
        for dx in (1, 2, 3, 0):
            for dy in range(SIDE):
                block = lax.rem(column // SIDE + dx, SIDE) * SIDE + lax.rem(column + dy, SIDE)
                weight = weight_ref[:, pl.ds(pl.multiple_of(block * share, share), share)]
                parts_ref[dx, dy] = jnp.dot(out, weight, preferred_element_type=jnp.float32)
            stores.append(pltpu.make_async_copy(parts_ref.at[dx], parts_any[dx], parts_sem.at[dx]))
            stores[-1].start()
        for store in stores:
            store.wait()


def add_kernel(a_ref, b_ref, c_ref, d_ref, *out_refs):
    for dy in range(SIDE):
        out_refs[dy][...] = (a_ref[dy] + b_ref[dy]) + (c_ref[dy] + d_ref[dy])


def residual_kernel(a_ref, b_ref, c_ref, d_ref, residual_ref, hsum_ref, square_ref):
    total = (a_ref[...] + b_ref[...]) + (c_ref[...] + d_ref[...])
    residual = residual_ref[...].astype(jnp.float32)
    hsum = jnp.concatenate([residual[r] for r in range(residual.shape[0])], axis=0) + total
    hsum_ref[...] = hsum
    square_ref[...] = jnp.broadcast_to(jnp.sum(hsum * hsum, axis=1, keepdims=True), square_ref.shape)


def norm_kernel(hsum_ref, a_ref, b_ref, c_ref, d_ref, gain_ref, normed_ref, residual_ref):
    total = (a_ref[...] + b_ref[...]) + (c_ref[...] + d_ref[...])
    hsum = hsum_ref[...]
    normed = hsum * lax.rsqrt(total[:, :1] / D + 1e-05) * gain_ref[...].astype(jnp.float32)
    for r in range(normed_ref.shape[0]):
        part = slice(r * STEPS, (r + 1) * STEPS)
        normed_ref[r] = normed[part].astype(jnp.bfloat16)
        residual_ref[r] = hsum[part].astype(jnp.bfloat16)


def widen_kernel(landed_any, arrived_any, in_ref, wide_ref, in_sem, out_sem):
    chunks, size = in_ref.shape[:2]
    loads, stores = [], []
    for n in range(chunks):
        part = pl.ds(n * size, size)
        loads.append(pltpu.make_async_copy(landed_any.at[part], in_ref.at[n], in_sem.at[n]))
        loads[n].start()
        stores.append(pltpu.make_async_copy(wide_ref.at[n], arrived_any.at[part], out_sem.at[n]))
    for n in range(chunks):
        loads[n].wait()
        wide_ref[n] = in_ref[n].astype(jnp.float32)
        stores[n].start()
    for store in stores:
        store.wait()


def shift_x(value, d):
    return lax.ppermute(
        value, "tensor", [(x * SIDE + y, ((x + d) % SIDE) * SIDE + y) for x in range(SIDE) for y in range(SIDE)]
    )


def shift_y(value, d):
    return lax.ppermute(
        value, "tensor", [(x * SIDE + y, x * SIDE + (y + d) % SIDE) for x in range(SIDE) for y in range(SIDE)]
    )


def here(value):
    return pltpu.with_memory_space_constraint(value, pltpu.HBM)


def params(mib=24):
    return pltpu.CompilerParams(vmem_limit_bytes=mib << 20)


def body(
    tokens_qkv,
    residual_in,
    state,
    decay_table,
    decay_index,
    active,
    move_slot,
    move_dest,
    norm_gain,
    out_weight,
):
    count, heads, width, _ = state.shape
    groups = lax.axis_size("batch")
    rows = count * STEPS
    share = residual_in.shape[2]
    f32, bf16 = jnp.float32, jnp.bfloat16
    pair = (CAP, heads, width, width)
    tokens = jnp.transpose(tokens_qkv, (0, 2, 1, 3))
    scalar_scratch = [
        pltpu.SMEM(decay_table.shape, f32),
        pltpu.SMEM(decay_index.shape, jnp.int32),
        pltpu.SMEM(active.shape, jnp.int32),
        pltpu.SMEM(move_slot.shape, jnp.int32),
        pltpu.SMEM(move_dest.shape, jnp.int32),
    ]
    scalars = (decay_table, decay_index, active, move_slot, move_dest)
    dma = pltpu.SemaphoreType.DMA

    moved = (groups * CAP,) + pair[1:]
    leaving = pl.pallas_call(
        leave_kernel,
        out_shape=pltpu.HBM(moved, bf16),
        in_specs=[HBM] * 7,
        out_specs=HBM,
        scratch_shapes=[
            *scalar_scratch,
            pltpu.VMEM(tokens.shape, bf16),
            pltpu.VMEM(state.shape, f32),
            pltpu.VMEM(moved, bf16),
            pltpu.SMEM((groups * CAP,), jnp.int32),
            dma((7,)),
            dma((groups,)),
        ],
        compiler_params=params(),
        cost_estimate=pl.CostEstimate(flops=32 * 20 * width * width, bytes_accessed=8 << 20, transcendentals=0),
        name="leave",
    )(*(here(value) for value in (*scalars, tokens, state)))
    landed = lax.all_to_all(leaving, "batch", split_axis=0, concat_axis=0, tiled=True)

    grid = 4
    new_state, *parts = pl.pallas_call(
        decode_kernel,
        grid=(grid,),
        out_shape=(
            pltpu.HBM(state.shape, f32),
            *[pltpu.HBM((SIDE, rows, share), f32)] * SIDE,
        ),
        in_specs=[HBM] * 5
        + [
            pl.BlockSpec((count // grid, 3, STEPS, heads * width), lambda i: (i, 0, 0, 0)),
            pl.BlockSpec((count // grid, heads, width, width), lambda i: (i, 0, 0, 0)),
            HBM,
            HBM,
        ],
        out_specs=(pl.BlockSpec((count // grid, heads, width, width), lambda i: (i, 0, 0, 0)), *[HBM] * SIDE),
        scratch_shapes=[
            *scalar_scratch,
            pltpu.SMEM((count,), jnp.int32),
            pltpu.VMEM((count, 8, heads * width), f32),
            pltpu.VMEM(out_weight.shape, bf16),
            pltpu.VMEM((SIDE, SIDE, rows, share), f32),
            dma((5,)),
            dma,
            dma((SIDE,)),
        ],
        compiler_params=params(),
        cost_estimate=pl.CostEstimate(flops=32 * 20 * width * width, bytes_accessed=8 << 20, transcendentals=0),
        name="decode",
    )(*(here(value) for value in (*scalars, tokens, state, out_weight, leaving)))

    lines = [parts[0]] + [shift_x(parts[d], d) for d in range(1, SIDE)]
    sums = pl.pallas_call(
        add_kernel,
        out_shape=[jax.ShapeDtypeStruct((rows, share), f32)] * SIDE,
        in_specs=[VMEM] * SIDE,
        out_specs=[VMEM] * SIDE,
        compiler_params=params(),
        name="add",
    )(*lines)
    terms = [sums[0]] + [shift_y(sums[d], d) for d in range(1, SIDE)]
    hsum, square = pl.pallas_call(
        residual_kernel,
        out_shape=(jax.ShapeDtypeStruct((rows, share), f32), jax.ShapeDtypeStruct((rows, W), f32)),
        in_specs=[VMEM] * (SIDE + 1),
        out_specs=(VMEM, VMEM),
        compiler_params=params(),
        name="residual",
    )(*terms, residual_in)
    square = square + (shift_x(square, 1) + shift_x(square, 2) + shift_x(square, 3))
    squares = [square] + [shift_y(square, d) for d in range(1, SIDE)]
    normed, residual_out = pl.pallas_call(
        norm_kernel,
        out_shape=[jax.ShapeDtypeStruct(residual_in.shape, bf16)] * 2,
        in_specs=[VMEM] * (SIDE + 2),
        out_specs=[VMEM] * 2,
        compiler_params=params(),
        name="norm",
    )(hsum, *squares, norm_gain.reshape(1, share))
    chunks = groups // 2
    arrived = pl.pallas_call(
        widen_kernel,
        out_shape=pltpu.HBM(moved, f32),
        in_specs=[pl.BlockSpec(memory_space=pl.ANY)],
        out_specs=HBM,
        scratch_shapes=[
            pltpu.VMEM((chunks, moved[0] // chunks) + pair[1:], bf16),
            pltpu.VMEM((chunks, moved[0] // chunks) + pair[1:], f32),
            dma((chunks,)),
            dma((chunks,)),
        ],
        compiler_params=params(),
        name="widen",
    )(landed)
    return (normed, residual_out, new_state, arrived)


def solution(mesh):
    return jax.shard_map(
        body,
        mesh=mesh,
        in_specs=(
            P("batch", None, None, "tensor"),
            P("batch", None, "tensor"),
            P("batch", "tensor", None, None),
            P(),
            P("tensor"),
            P("batch"),
            P("batch", None),
            P("batch", None),
            P("tensor"),
            P("tensor", None),
        ),
        out_specs=(
            P("batch", None, "tensor"),
            P("batch", None, "tensor"),
            P("batch", "tensor", None, None),
            P("batch", "tensor", None, None),
        ),
        check_vma=False,
    )
```

```python
import jax
import jax.numpy as jnp
from jax import lax
from jax.experimental import pallas as pl
from jax.experimental.pallas import tpu as pltpu
from jax.sharding import PartitionSpec as P

D = 8192
STEPS = 2
PAIR = 2
CAP = 2
SIDE = 4
W = 128

SMEM = pl.BlockSpec(memory_space=pltpu.SMEM)
VMEM = pl.BlockSpec(memory_space=pltpu.VMEM)
HBM = pl.BlockSpec(memory_space=pltpu.HBM)


def decay(table_ref, index_ref, h):
    return table_ref[index_ref[h]]


def make_masks(slots, heads, extra):
    block = 4 * heads
    shape = (slots * block + extra, slots * heads * W)
    row = lax.broadcasted_iota(jnp.int32, shape, 0)
    lane = lax.broadcasted_iota(jnp.int32, shape, 1)
    return row % 4, (row // 4) == (lane // W), row


def factors(keys, values, gamma, masks, queries=None):
    term, own, row = masks
    slots, heads = len(keys), keys[0].shape[1] // W
    key = jnp.concatenate(keys, axis=1)
    first = gamma * key[0:1]
    hi = first.astype(jnp.bfloat16).astype(jnp.float32)
    mid = (first - hi).astype(jnp.bfloat16).astype(jnp.float32)
    low = first - hi - mid
    left = jnp.where(term == 0, hi, jnp.where(term == 1, mid, jnp.where(term == 2, low, key[1:2])))
    left = jnp.where(own, left, 0.0)
    line = lax.broadcasted_iota(jnp.int32, (row.shape[0], W), 0)
    right = jnp.zeros((row.shape[0], W), jnp.float32)
    for s in range(slots):
        for h in range(heads):
            at = 4 * (s * heads + h)
            part = values[s][:, h * W : (h + 1) * W]
            right = jnp.where((line >= at) & (line < at + 3), part[0:1], right)
            right = jnp.where(line == at + 3, part[1:2], right)
    if queries is not None:
        at = 4 * slots * heads
        query = jnp.concatenate(queries, axis=1)
        left = jnp.where(row == at, query[0:1], jnp.where(row == at + 1, query[1:2], left))
        ones = [jnp.where(line == at + t, 1.0, 0.0) for t in range(STEPS)]
        right = jnp.concatenate([right, *ones], axis=1)
    return left, right


def gamma_row(table_ref, index_ref, slots, heads):
    lane = lax.broadcasted_iota(jnp.int32, (1, slots * heads * W), 1)
    out = jnp.zeros(lane.shape, jnp.float32)
    for h in range(heads):
        out = jnp.where((lane // W) % heads == h, decay(table_ref, index_ref, h), out)
    return out


def outer(left, right):
    return lax.dot_general(
        left.astype(jnp.bfloat16),
        right.astype(jnp.bfloat16),
        (((0,), (0,)), ((), ())),
        preferred_element_type=jnp.float32,
    )


def leave_kernel(
    table_any,
    index_any,
    active_any,
    slot_any,
    dest_any,
    tok_any,
    state_any,
    out_any,
    table_ref,
    index_ref,
    active_ref,
    slot_ref,
    dest_ref,
    tok_ref,
    state_ref,
    buf_ref,
    map_ref,
    in_sem,
    out_sem,
):
    me = lax.axis_index("batch")
    entries = slot_ref.shape[1]
    heads = state_ref.shape[1]
    groups = map_ref.shape[0] // CAP
    pairs = (
        (state_any, state_ref),
        (tok_any, tok_ref),
        (slot_any, slot_ref),
        (dest_any, dest_ref),
        (active_any, active_ref),
        (table_any, table_ref),
        (index_any, index_ref),
    )
    loads = [pltpu.make_async_copy(a, b, in_sem.at[n]) for n, (a, b) in enumerate(pairs)]
    for load in loads:
        load.start()
    for n in range(map_ref.shape[0]):
        map_ref[n] = -1
    for load in loads[2:]:
        load.wait()

    def entry(j, carry):
        dest = dest_ref[0, j]
        base = dest * CAP
        taken = jnp.where(map_ref[base] >= 0, 1, 0)

        @pl.when(dest != me)
        def _():
            map_ref[base + taken] = slot_ref[0, j]

        return carry

    lax.fori_loop(0, entries, entry, 0)
    loads[1].wait()
    loads[0].wait()
    def store_of(n):
        part = pl.ds(n * CAP, CAP)
        return pltpu.make_async_copy(buf_ref.at[part], out_any.at[part], out_sem.at[n])

    masks = make_masks(CAP, heads, 0)
    gamma = gamma_row(table_ref, index_ref, CAP, heads)

    def fill(n, carry):
        slots, keys, values, keeps = [], [], [], []
        for position in range(CAP):
            found = map_ref[n * CAP + position]
            slot = jnp.maximum(found, 0)
            on = active_ref[slot] > 0
            here = jnp.where(found >= 0, 1.0, 0.0)
            tokens = tok_ref[slot].astype(jnp.float32)
            slots.append(slot)
            keys.append(tokens[1] * jnp.where(on, here, 0.0))
            values.append(tokens[2])
            keeps.append([here * jnp.where(on, decay(table_ref, index_ref, h) ** 2, 1.0) for h in range(heads)])
        added = outer(*factors(keys, values, gamma, masks))
        for position in range(CAP):
            for h in range(heads):
                at = (position * heads + h) * W
                final = keeps[position][h] * state_ref[slots[position], h] + added[at : at + W]
                buf_ref[n * CAP + position, h] = final.astype(jnp.bfloat16)
        store_of(n).start()
        return carry

    lax.fori_loop(0, groups, fill, 0, unroll=groups)
    for n in range(groups):
        store_of(n).wait()


def decode_kernel(
    table_any,
    index_any,
    active_any,
    slot_any,
    dest_any,
    tok_any,
    state_any,
    weight_any,
    after_any,
    new_any,
    part0_ref,
    part1_any,
    part2_any,
    part3_any,
    table_ref,
    index_ref,
    active_ref,
    slot_ref,
    dest_ref,
    tok_ref,
    state_ref,
    new_ref,
    gone_ref,
    heads_ref,
    weight_ref,
    parts_ref,
    scalar_sem,
    weight_sem,
    parts_sem,
    state_sem,
    new_sem,
):
    parts_any = (part0_ref, part1_any, part2_any, part3_any)
    me = lax.axis_index("batch")
    entries = slot_ref.shape[1]
    heads = state_ref.shape[1]
    count = state_ref.shape[0]
    pairs = (
        (table_any, table_ref),
        (index_any, index_ref),
        (active_any, active_ref),
        (slot_any, slot_ref),
        (dest_any, dest_ref),
        (tok_any, tok_ref),
    )
    copies = [pltpu.make_async_copy(a, b, scalar_sem.at[n]) for n, (a, b) in enumerate(pairs)]
    for copy in copies:
        copy.start()
    loads, stores = [], []
    for n in range(count // PAIR):
        part = pl.ds(n * PAIR, PAIR)
        loads.append(pltpu.make_async_copy(state_any.at[part], state_ref.at[part], state_sem.at[n]))
        stores.append(pltpu.make_async_copy(new_ref.at[part], new_any.at[part], new_sem.at[n]))
        loads[n].start()
    load = pltpu.make_async_copy(weight_any, weight_ref, weight_sem)
    load.start()
    for copy in copies:
        copy.wait()
    for s in range(count):
        gone_ref[s] = 0
    for j in range(entries):
        slot = slot_ref[0, j]
        gone_ref[slot] = gone_ref[slot] + jnp.where(dest_ref[0, j] != me, 1, 0)

    row = lax.broadcasted_iota(jnp.int32, (8, W), 0)
    masks = make_masks(PAIR, heads, 16)
    gammas = gamma_row(table_ref, index_ref, PAIR, heads)
    for part in loads:
        part.wait()
    for pair in range(count // PAIR):
        at = [pair * PAIR + n for n in range(PAIR)]
        tokens = [tok_ref[b].astype(jnp.float32) for b in at]
        on = [active_ref[b] > 0 for b in at]
        live = [jnp.where(gone_ref[b] > 0, 0.0, 1.0) for b in at]
        keys = [token[1] * jnp.where(flag, 1.0, 0.0) for token, flag in zip(tokens, on)]
        mixed = outer(*factors(keys, [token[2] for token in tokens], gammas, masks, [token[0] for token in tokens]))
        for n, b in enumerate(at):
            for h in range(heads):
                part = slice(h * W, (h + 1) * W)
                q, k, v = tokens[n][0][:, part], keys[n][:, part], tokens[n][2][:, part]
                gamma = decay(table_ref, index_ref, h)
                top = (n * heads + h) * W
                before = state_ref[b, h]
                raw1 = gamma * jnp.sum(mixed[top : top + W, W : 2 * W] * before, axis=0, keepdims=True)
                raw1 = raw1 + jnp.sum(q[0:1] * k[0:1], axis=1, keepdims=True) * v[0:1]
                final = jnp.where(on[n], gamma * gamma, 1.0) * before + mixed[top : top + W, :W]
                raw2 = jnp.sum(mixed[top : top + W, 2 * W :] * final, axis=0, keepdims=True)
                raw = jnp.where(row == 0, raw1, jnp.where(row == 1, raw2, 0.0))
                scaled = raw * lax.rsqrt(jnp.mean(raw * raw, axis=1, keepdims=True) + 1e-06)
                heads_ref[b, :, part] = jnp.where(on[n], scaled, 0.0)
                new_ref[b, h] = live[n] * final
        stores[pair].start()

    count, padded, depth = heads_ref.shape
    rows = count * STEPS
    line = lax.broadcasted_iota(jnp.int32, (rows, count * padded), 0)
    source = lax.broadcasted_iota(jnp.int32, (rows, count * padded), 1)
    pick = jnp.where(source == (line // STEPS) * padded + line % STEPS, 1.0, 0.0).astype(jnp.bfloat16)
    out = heads_ref[...].reshape(count * padded, depth).astype(jnp.bfloat16)
    out = jnp.dot(pick, out, preferred_element_type=jnp.float32).astype(jnp.bfloat16)
    load.wait()
    share = parts_ref.shape[3]
    column = lax.axis_index("tensor")
    sends = []
    for dx in (1, 2, 3, 0):
        for dy in range(SIDE):
            block = lax.rem(column // SIDE + dx, SIDE) * SIDE + lax.rem(column + dy, SIDE)
            weight = weight_ref[:, pl.ds(pl.multiple_of(block * share, share), share)]
            target = parts_ref.at[dx - 1, dy] if dx else part0_ref.at[dy]
            target[...] = jnp.dot(out, weight, preferred_element_type=jnp.float32)
        if dx:
            sends.append(pltpu.make_async_copy(parts_ref.at[dx - 1], parts_any[dx], parts_sem.at[dx - 1]))
            sends[-1].start()
    for store in [*stores, *sends]:
        store.wait()


def add_kernel(a_ref, b_ref, c_ref, d_ref, *out_refs):
    for dy in range(SIDE):
        out_refs[dy][...] = (a_ref[dy] + b_ref[dy]) + (c_ref[dy] + d_ref[dy])


def residual_kernel(a_ref, b_ref, c_ref, d_ref, residual_ref, hsum_ref, square_ref):
    total = (a_ref[...] + b_ref[...]) + (c_ref[...] + d_ref[...])
    residual = residual_ref[...].astype(jnp.float32)
    hsum = jnp.concatenate([residual[r] for r in range(residual.shape[0])], axis=0) + total
    hsum_ref[...] = hsum
    square_ref[...] = jnp.broadcast_to(jnp.sum(hsum * hsum, axis=1, keepdims=True), square_ref.shape)


def norm_kernel(hsum_ref, a_ref, b_ref, c_ref, d_ref, gain_ref, normed_ref, residual_ref):
    total = (a_ref[...] + b_ref[...]) + (c_ref[...] + d_ref[...])
    hsum = hsum_ref[...]
    normed = hsum * lax.rsqrt(total[:, :1] / D + 1e-05) * gain_ref[...].astype(jnp.float32)
    for r in range(normed_ref.shape[0]):
        part = slice(r * STEPS, (r + 1) * STEPS)
        normed_ref[r] = normed[part].astype(jnp.bfloat16)
        residual_ref[r] = hsum[part].astype(jnp.bfloat16)


def widen_kernel(landed_ref, arrived_any, wide_ref, out_sem):
    chunks, size = wide_ref.shape[:2]
    stores = []
    for n in range(chunks):
        part = pl.ds(n * size, size)
        wide_ref[n] = landed_ref[part].astype(jnp.float32)
        stores.append(pltpu.make_async_copy(wide_ref.at[n], arrived_any.at[part], out_sem.at[n]))
        stores[n].start()
    for store in stores:
        store.wait()


def shift_x(value, d):
    return lax.ppermute(
        value, "tensor", [(x * SIDE + y, ((x + d) % SIDE) * SIDE + y) for x in range(SIDE) for y in range(SIDE)]
    )


def shift_y(value, d):
    return lax.ppermute(
        value, "tensor", [(x * SIDE + y, x * SIDE + (y + d) % SIDE) for x in range(SIDE) for y in range(SIDE)]
    )


def here(value):
    return pltpu.with_memory_space_constraint(value, pltpu.HBM)


def params(mib=24):
    return pltpu.CompilerParams(vmem_limit_bytes=mib << 20)


def body(
    tokens_qkv,
    residual_in,
    state,
    decay_table,
    decay_index,
    active,
    move_slot,
    move_dest,
    norm_gain,
    out_weight,
):
    count, heads, width, _ = state.shape
    groups = lax.axis_size("batch")
    rows = count * STEPS
    share = residual_in.shape[2]
    f32, bf16 = jnp.float32, jnp.bfloat16
    pair = (CAP, heads, width, width)
    tokens = jnp.transpose(tokens_qkv, (0, 2, 1, 3))
    scalar_scratch = [
        pltpu.SMEM(decay_table.shape, f32),
        pltpu.SMEM(decay_index.shape, jnp.int32),
        pltpu.SMEM(active.shape, jnp.int32),
        pltpu.SMEM(move_slot.shape, jnp.int32),
        pltpu.SMEM(move_dest.shape, jnp.int32),
    ]
    scalars = (decay_table, decay_index, active, move_slot, move_dest)
    dma = pltpu.SemaphoreType.DMA

    moved = (groups * CAP,) + pair[1:]
    leaving = pl.pallas_call(
        leave_kernel,
        out_shape=pltpu.HBM(moved, bf16),
        in_specs=[HBM] * 7,
        out_specs=HBM,
        scratch_shapes=[
            *scalar_scratch,
            pltpu.VMEM(tokens.shape, bf16),
            pltpu.VMEM(state.shape, f32),
            pltpu.VMEM(moved, bf16),
            pltpu.SMEM((groups * CAP,), jnp.int32),
            dma((7,)),
            dma((groups,)),
        ],
        compiler_params=params(),
        cost_estimate=pl.CostEstimate(flops=32 * 20 * width * width, bytes_accessed=8 << 20, transcendentals=0),
        name="leave",
    )(*(here(value) for value in (*scalars, tokens, state)))
    landed = lax.all_to_all(leaving, "batch", split_axis=0, concat_axis=0, tiled=True)

    new_state, *parts = pl.pallas_call(
        decode_kernel,
        out_shape=(
            pltpu.HBM(state.shape, f32),
            jax.ShapeDtypeStruct((SIDE, rows, share), f32),
            *[pltpu.HBM((SIDE, rows, share), f32)] * (SIDE - 1),
        ),
        in_specs=[HBM] * 9,
        out_specs=[HBM, VMEM] + [HBM] * (SIDE - 1),
        scratch_shapes=[
            *scalar_scratch,
            pltpu.VMEM(tokens.shape, bf16),
            pltpu.VMEM(state.shape, f32),
            pltpu.VMEM(state.shape, f32),
            pltpu.SMEM((count,), jnp.int32),
            pltpu.VMEM((count, 8, heads * width), f32),
            pltpu.VMEM(out_weight.shape, bf16),
            pltpu.VMEM((SIDE - 1, SIDE, rows, share), f32),
            dma((6,)),
            dma,
            dma((SIDE - 1,)),
            dma((count // PAIR,)),
            dma((count // PAIR,)),
        ],
        compiler_params=params(),
        cost_estimate=pl.CostEstimate(flops=32 * 20 * width * width, bytes_accessed=8 << 20, transcendentals=0),
        name="decode",
    )(*(here(value) for value in (*scalars, tokens, state, out_weight, leaving)))

    lines = [parts[0]] + [shift_x(parts[d], d) for d in range(1, SIDE)]
    sums = pl.pallas_call(
        add_kernel,
        out_shape=[jax.ShapeDtypeStruct((rows, share), f32)] * SIDE,
        in_specs=[VMEM] * SIDE,
        out_specs=[VMEM] * SIDE,
        compiler_params=params(),
        name="add",
    )(*lines)
    terms = [sums[0]] + [shift_y(sums[d], d) for d in range(1, SIDE)]
    hsum, square = pl.pallas_call(
        residual_kernel,
        out_shape=(jax.ShapeDtypeStruct((rows, share), f32), jax.ShapeDtypeStruct((rows, W), f32)),
        in_specs=[VMEM] * (SIDE + 1),
        out_specs=(VMEM, VMEM),
        compiler_params=params(),
        name="residual",
    )(*terms, residual_in)
    square = square + (shift_x(square, 1) + shift_x(square, 2) + shift_x(square, 3))
    squares = [square] + [shift_y(square, d) for d in range(1, SIDE)]
    normed, residual_out = pl.pallas_call(
        norm_kernel,
        out_shape=[jax.ShapeDtypeStruct(residual_in.shape, bf16)] * 2,
        in_specs=[VMEM] * (SIDE + 2),
        out_specs=[VMEM] * 2,
        compiler_params=params(),
        name="norm",
    )(hsum, *squares, norm_gain.reshape(1, share))
    chunks = groups // 2
    arrived = pl.pallas_call(
        widen_kernel,
        out_shape=pltpu.HBM(moved, f32),
        in_specs=[VMEM],
        out_specs=HBM,
        scratch_shapes=[pltpu.VMEM((chunks, moved[0] // chunks) + pair[1:], f32), dma((chunks,))],
        compiler_params=params(),
        name="widen",
    )(landed)
    return (normed, residual_out, new_state, arrived)


def solution(mesh):
    return jax.shard_map(
        body,
        mesh=mesh,
        in_specs=(
            P("batch", None, None, "tensor"),
            P("batch", None, "tensor"),
            P("batch", "tensor", None, None),
            P(),
            P("tensor"),
            P("batch"),
            P("batch", None),
            P("batch", None),
            P("tensor"),
            P("tensor", None),
        ),
        out_specs=(
            P("batch", None, "tensor"),
            P("batch", None, "tensor"),
            P("batch", "tensor", None, None),
            P("batch", "tensor", None, None),
        ),
        check_vma=False,
    )
```

```python
import jax
import jax.numpy as jnp
from jax import lax
from jax.experimental import pallas as pl
from jax.experimental.pallas import tpu as pltpu
from jax.sharding import PartitionSpec as P

D = 8192
STEPS = 2
PAIR = 2
CAP = 2
SIDE = 4
W = 128

SMEM = pl.BlockSpec(memory_space=pltpu.SMEM)
VMEM = pl.BlockSpec(memory_space=pltpu.VMEM)
HBM = pl.BlockSpec(memory_space=pltpu.HBM)


def decay(table_ref, index_ref, h):
    return table_ref[index_ref[h]]


def make_masks(slots, heads, extra):
    block = 4 * heads
    shape = (slots * block + extra, slots * heads * W)
    row = lax.broadcasted_iota(jnp.int32, shape, 0)
    lane = lax.broadcasted_iota(jnp.int32, shape, 1)
    return row % 4, (row // 4) == (lane // W), row


def factors(keys, values, gamma, masks, queries=None):
    term, own, row = masks
    slots, heads = len(keys), keys[0].shape[1] // W
    key = jnp.concatenate(keys, axis=1)
    first = gamma * key[0:1]
    hi = first.astype(jnp.bfloat16).astype(jnp.float32)
    mid = (first - hi).astype(jnp.bfloat16).astype(jnp.float32)
    low = first - hi - mid
    left = jnp.where(term == 0, hi, jnp.where(term == 1, mid, jnp.where(term == 2, low, key[1:2])))
    left = jnp.where(own, left, 0.0)
    line = lax.broadcasted_iota(jnp.int32, (row.shape[0], W), 0)
    right = jnp.zeros((row.shape[0], W), jnp.float32)
    for s in range(slots):
        for h in range(heads):
            at = 4 * (s * heads + h)
            part = values[s][:, h * W : (h + 1) * W]
            right = jnp.where((line >= at) & (line < at + 3), part[0:1], right)
            right = jnp.where(line == at + 3, part[1:2], right)
    if queries is not None:
        at = 4 * slots * heads
        query = jnp.concatenate(queries, axis=1)
        left = jnp.where(row == at, query[0:1], jnp.where(row == at + 1, query[1:2], left))
        ones = [jnp.where(line == at + t, 1.0, 0.0) for t in range(STEPS)]
        right = jnp.concatenate([right, *ones], axis=1)
    return left, right


def gamma_row(table_ref, index_ref, slots, heads):
    lane = lax.broadcasted_iota(jnp.int32, (1, slots * heads * W), 1)
    out = jnp.zeros(lane.shape, jnp.float32)
    for h in range(heads):
        out = jnp.where((lane // W) % heads == h, decay(table_ref, index_ref, h), out)
    return out


def outer(left, right):
    return lax.dot_general(
        left.astype(jnp.bfloat16),
        right.astype(jnp.bfloat16),
        (((0,), (0,)), ((), ())),
        preferred_element_type=jnp.float32,
    )


def leave_kernel(
    table_any,
    index_any,
    active_any,
    slot_any,
    dest_any,
    tok_any,
    state_any,
    out_any,
    table_ref,
    index_ref,
    active_ref,
    slot_ref,
    dest_ref,
    tok_ref,
    state_ref,
    buf_ref,
    row_ref,
    in_sem,
    state_sem,
    out_sem,
):
    me = lax.axis_index("batch")
    count, heads = state_ref.shape[:2]
    entries = slot_ref.shape[1]
    spare = out_any.shape[0]
    pairs = (
        (slot_any, slot_ref),
        (dest_any, dest_ref),
        (active_any, active_ref),
        (table_any, table_ref),
        (index_any, index_ref),
        (tok_any, tok_ref),
    )
    copies = [pltpu.make_async_copy(a, b, in_sem.at[n]) for n, (a, b) in enumerate(pairs)]
    for copy in copies:
        copy.start()
    loads = []
    for n in range(count // PAIR):
        part = pl.ds(n * PAIR, PAIR)
        loads.append(pltpu.make_async_copy(state_any.at[part], state_ref.at[part], state_sem.at[n]))
        loads[n].start()
    for n in range(spare):
        row_ref[n] = count
    buf_ref[count] = jnp.zeros(buf_ref.shape[1:], buf_ref.dtype)
    for copy in copies:
        copy.wait()
    for j in range(entries):
        dest = dest_ref[0, j]
        position = jnp.where(row_ref[dest * CAP] < count, 1, 0)
        row_ref[jnp.where(dest != me, dest * CAP + position, spare)] = slot_ref[0, j]

    def store_of(n, slot):
        return pltpu.make_async_copy(buf_ref.at[pl.ds(slot, 1)], out_any.at[pl.ds(n, 1)], out_sem.at[n])

    for n in range(spare):

        @pl.when(row_ref[n] >= count)
        def _(n=n):
            store_of(n, count).start()

    masks = make_masks(PAIR, heads, 0)
    gammas = gamma_row(table_ref, index_ref, PAIR, heads)
    for load in loads:
        load.wait()
    for pair in range(count // PAIR):
        slots = [pair * PAIR + n for n in range(PAIR)]
        tokens = [tok_ref[slot].astype(jnp.float32) for slot in slots]
        on = [active_ref[slot] > 0 for slot in slots]
        keys = [token[1] * jnp.where(flag, 1.0, 0.0) for token, flag in zip(tokens, on)]
        added = outer(*factors(keys, [token[2] for token in tokens], gammas, masks))
        for n, slot in enumerate(slots):
            for h in range(heads):
                keep = jnp.where(on[n], decay(table_ref, index_ref, h) ** 2, 1.0)
                top = (n * heads + h) * W
                final = keep * state_ref[slot, h] + added[top : top + W]
                buf_ref[slot, h] = final.astype(jnp.bfloat16)
    for n in range(spare):

        @pl.when(row_ref[n] < count)
        def _(n=n):
            store_of(n, row_ref[n]).start()

    for n in range(spare):
        store_of(n, 0).wait()


def decode_kernel(
    table_any,
    index_any,
    active_any,
    slot_any,
    dest_any,
    tok_any,
    state_any,
    weight_any,
    after_any,
    new_any,
    part0_ref,
    part1_any,
    part2_any,
    part3_any,
    table_ref,
    index_ref,
    active_ref,
    slot_ref,
    dest_ref,
    tok_ref,
    state_ref,
    new_ref,
    gone_ref,
    heads_ref,
    weight_ref,
    parts_ref,
    scalar_sem,
    weight_sem,
    parts_sem,
    state_sem,
    new_sem,
):
    parts_any = (part0_ref, part1_any, part2_any, part3_any)
    me = lax.axis_index("batch")
    entries = slot_ref.shape[1]
    heads = state_ref.shape[1]
    count = state_ref.shape[0]
    pairs = (
        (table_any, table_ref),
        (index_any, index_ref),
        (active_any, active_ref),
        (slot_any, slot_ref),
        (dest_any, dest_ref),
        (tok_any, tok_ref),
    )
    copies = [pltpu.make_async_copy(a, b, scalar_sem.at[n]) for n, (a, b) in enumerate(pairs)]
    for copy in copies:
        copy.start()
    loads, stores = [], []
    for n in range(count // PAIR):
        part = pl.ds(n * PAIR, PAIR)
        loads.append(pltpu.make_async_copy(state_any.at[part], state_ref.at[part], state_sem.at[n]))
        stores.append(pltpu.make_async_copy(new_ref.at[part], new_any.at[part], new_sem.at[n]))
        loads[n].start()
    load = pltpu.make_async_copy(weight_any, weight_ref, weight_sem)
    load.start()
    for copy in copies:
        copy.wait()
    for s in range(count):
        gone_ref[s] = 0
    for j in range(entries):
        slot = slot_ref[0, j]
        gone_ref[slot] = gone_ref[slot] + jnp.where(dest_ref[0, j] != me, 1, 0)

    row = lax.broadcasted_iota(jnp.int32, (8, W), 0)
    masks = make_masks(PAIR, heads, 16)
    gammas = gamma_row(table_ref, index_ref, PAIR, heads)
    for part in loads:
        part.wait()
    for pair in range(count // PAIR):
        at = [pair * PAIR + n for n in range(PAIR)]
        tokens = [tok_ref[b].astype(jnp.float32) for b in at]
        on = [active_ref[b] > 0 for b in at]
        live = [jnp.where(gone_ref[b] > 0, 0.0, 1.0) for b in at]
        keys = [token[1] * jnp.where(flag, 1.0, 0.0) for token, flag in zip(tokens, on)]
        mixed = outer(*factors(keys, [token[2] for token in tokens], gammas, masks, [token[0] for token in tokens]))
        for n, b in enumerate(at):
            for h in range(heads):
                part = slice(h * W, (h + 1) * W)
                q, k, v = tokens[n][0][:, part], keys[n][:, part], tokens[n][2][:, part]
                gamma = decay(table_ref, index_ref, h)
                top = (n * heads + h) * W
                before = state_ref[b, h]
                raw1 = gamma * jnp.sum(mixed[top : top + W, W : 2 * W] * before, axis=0, keepdims=True)
                raw1 = raw1 + jnp.sum(q[0:1] * k[0:1], axis=1, keepdims=True) * v[0:1]
                final = jnp.where(on[n], gamma * gamma, 1.0) * before + mixed[top : top + W, :W]
                raw2 = jnp.sum(mixed[top : top + W, 2 * W :] * final, axis=0, keepdims=True)
                raw = jnp.where(row == 0, raw1, jnp.where(row == 1, raw2, 0.0))
                scaled = raw * lax.rsqrt(jnp.mean(raw * raw, axis=1, keepdims=True) + 1e-06)
                heads_ref[b, :, part] = jnp.where(on[n], scaled, 0.0)
                new_ref[b, h] = live[n] * final
        stores[pair].start()

    count, padded, depth = heads_ref.shape
    rows = count * STEPS
    line = lax.broadcasted_iota(jnp.int32, (rows, count * padded), 0)
    source = lax.broadcasted_iota(jnp.int32, (rows, count * padded), 1)
    pick = jnp.where(source == (line // STEPS) * padded + line % STEPS, 1.0, 0.0).astype(jnp.bfloat16)
    out = heads_ref[...].reshape(count * padded, depth).astype(jnp.bfloat16)
    out = jnp.dot(pick, out, preferred_element_type=jnp.float32).astype(jnp.bfloat16)
    load.wait()
    share = parts_ref.shape[3]
    column = lax.axis_index("tensor")
    sends = []
    for dx in (1, 2, 3, 0):
        for dy in range(SIDE):
            block = lax.rem(column // SIDE + dx, SIDE) * SIDE + lax.rem(column + dy, SIDE)
            weight = weight_ref[:, pl.ds(pl.multiple_of(block * share, share), share)]
            target = parts_ref.at[dx - 1, dy] if dx else part0_ref.at[dy]
            target[...] = jnp.dot(out, weight, preferred_element_type=jnp.float32)
        if dx:
            sends.append(pltpu.make_async_copy(parts_ref.at[dx - 1], parts_any[dx], parts_sem.at[dx - 1]))
            sends[-1].start()
    for store in [*stores, *sends]:
        store.wait()


def add_kernel(a_ref, b_ref, c_ref, d_ref, *out_refs):
    for dy in range(SIDE):
        out_refs[dy][...] = (a_ref[dy] + b_ref[dy]) + (c_ref[dy] + d_ref[dy])


def residual_kernel(a_ref, b_ref, c_ref, d_ref, residual_ref, hsum_ref, square_ref):
    total = (a_ref[...] + b_ref[...]) + (c_ref[...] + d_ref[...])
    residual = residual_ref[...].astype(jnp.float32)
    hsum = jnp.concatenate([residual[r] for r in range(residual.shape[0])], axis=0) + total
    hsum_ref[...] = hsum
    square_ref[...] = jnp.broadcast_to(jnp.sum(hsum * hsum, axis=1, keepdims=True), square_ref.shape)


def norm_kernel(hsum_ref, a_ref, b_ref, c_ref, d_ref, gain_ref, normed_ref, residual_ref):
    total = (a_ref[...] + b_ref[...]) + (c_ref[...] + d_ref[...])
    hsum = hsum_ref[...]
    normed = hsum * lax.rsqrt(total[:, :1] / D + 1e-05) * gain_ref[...].astype(jnp.float32)
    for r in range(normed_ref.shape[0]):
        part = slice(r * STEPS, (r + 1) * STEPS)
        normed_ref[r] = normed[part].astype(jnp.bfloat16)
        residual_ref[r] = hsum[part].astype(jnp.bfloat16)


def widen_kernel(landed_ref, arrived_any, wide_ref, out_sem):
    chunks, size = wide_ref.shape[:2]
    stores = []
    for n in range(chunks):
        part = pl.ds(n * size, size)
        wide_ref[n] = landed_ref[part].astype(jnp.float32)
        stores.append(pltpu.make_async_copy(wide_ref.at[n], arrived_any.at[part], out_sem.at[n]))
        stores[n].start()
    for store in stores:
        store.wait()


def shift_x(value, d):
    return lax.ppermute(
        value, "tensor", [(x * SIDE + y, ((x + d) % SIDE) * SIDE + y) for x in range(SIDE) for y in range(SIDE)]
    )


def shift_y(value, d):
    return lax.ppermute(
        value, "tensor", [(x * SIDE + y, x * SIDE + (y + d) % SIDE) for x in range(SIDE) for y in range(SIDE)]
    )


def here(value):
    return pltpu.with_memory_space_constraint(value, pltpu.HBM)


def params(mib=24):
    return pltpu.CompilerParams(vmem_limit_bytes=mib << 20)


def body(
    tokens_qkv,
    residual_in,
    state,
    decay_table,
    decay_index,
    active,
    move_slot,
    move_dest,
    norm_gain,
    out_weight,
):
    count, heads, width, _ = state.shape
    groups = lax.axis_size("batch")
    rows = count * STEPS
    share = residual_in.shape[2]
    f32, bf16 = jnp.float32, jnp.bfloat16
    pair = (CAP, heads, width, width)
    tokens = jnp.transpose(tokens_qkv, (0, 2, 1, 3))
    scalar_scratch = [
        pltpu.SMEM(decay_table.shape, f32),
        pltpu.SMEM(decay_index.shape, jnp.int32),
        pltpu.SMEM(active.shape, jnp.int32),
        pltpu.SMEM(move_slot.shape, jnp.int32),
        pltpu.SMEM(move_dest.shape, jnp.int32),
    ]
    scalars = (decay_table, decay_index, active, move_slot, move_dest)
    dma = pltpu.SemaphoreType.DMA

    moved = (groups * CAP,) + pair[1:]
    leaving = pl.pallas_call(
        leave_kernel,
        out_shape=pltpu.HBM(moved, bf16),
        in_specs=[HBM] * 7,
        out_specs=HBM,
        scratch_shapes=[
            *scalar_scratch,
            pltpu.VMEM(tokens.shape, bf16),
            pltpu.VMEM(state.shape, f32),
            pltpu.VMEM((count + 1,) + pair[1:], bf16),
            pltpu.SMEM((moved[0] + 1,), jnp.int32),
            dma((6,)),
            dma((count // PAIR,)),
            dma((moved[0],)),
        ],
        compiler_params=params(),
        cost_estimate=pl.CostEstimate(flops=32 * 20 * width * width, bytes_accessed=8 << 20, transcendentals=0),
        name="leave",
    )(*(here(value) for value in (*scalars, tokens, state)))
    landed = lax.all_to_all(leaving, "batch", split_axis=0, concat_axis=0, tiled=True)

    new_state, *parts = pl.pallas_call(
        decode_kernel,
        out_shape=(
            pltpu.HBM(state.shape, f32),
            jax.ShapeDtypeStruct((SIDE, rows, share), f32),
            *[pltpu.HBM((SIDE, rows, share), f32)] * (SIDE - 1),
        ),
        in_specs=[HBM] * 9,
        out_specs=[HBM, VMEM] + [HBM] * (SIDE - 1),
        scratch_shapes=[
            *scalar_scratch,
            pltpu.VMEM(tokens.shape, bf16),
            pltpu.VMEM(state.shape, f32),
            pltpu.VMEM(state.shape, f32),
            pltpu.SMEM((count,), jnp.int32),
            pltpu.VMEM((count, 8, heads * width), f32),
            pltpu.VMEM(out_weight.shape, bf16),
            pltpu.VMEM((SIDE - 1, SIDE, rows, share), f32),
            dma((6,)),
            dma,
            dma((SIDE - 1,)),
            dma((count // PAIR,)),
            dma((count // PAIR,)),
        ],
        compiler_params=params(),
        cost_estimate=pl.CostEstimate(flops=32 * 20 * width * width, bytes_accessed=8 << 20, transcendentals=0),
        name="decode",
    )(*(here(value) for value in (*scalars, tokens, state, out_weight, leaving)))

    lines = [parts[0]] + [shift_x(parts[d], d) for d in range(1, SIDE)]
    sums = pl.pallas_call(
        add_kernel,
        out_shape=[jax.ShapeDtypeStruct((rows, share), f32)] * SIDE,
        in_specs=[VMEM] * SIDE,
        out_specs=[VMEM] * SIDE,
        compiler_params=params(),
        name="add",
    )(*lines)
    terms = [sums[0]] + [shift_y(sums[d], d) for d in range(1, SIDE)]
    hsum, square = pl.pallas_call(
        residual_kernel,
        out_shape=(jax.ShapeDtypeStruct((rows, share), f32), jax.ShapeDtypeStruct((rows, W), f32)),
        in_specs=[VMEM] * (SIDE + 1),
        out_specs=(VMEM, VMEM),
        compiler_params=params(),
        name="residual",
    )(*terms, residual_in)
    square = square + (shift_x(square, 1) + shift_x(square, 2) + shift_x(square, 3))
    squares = [square] + [shift_y(square, d) for d in range(1, SIDE)]
    normed, residual_out = pl.pallas_call(
        norm_kernel,
        out_shape=[jax.ShapeDtypeStruct(residual_in.shape, bf16)] * 2,
        in_specs=[VMEM] * (SIDE + 2),
        out_specs=[VMEM] * 2,
        compiler_params=params(),
        name="norm",
    )(hsum, *squares, norm_gain.reshape(1, share))
    chunks = groups // 2
    arrived = pl.pallas_call(
        widen_kernel,
        out_shape=pltpu.HBM(moved, f32),
        in_specs=[VMEM],
        out_specs=HBM,
        scratch_shapes=[pltpu.VMEM((chunks, moved[0] // chunks) + pair[1:], f32), dma((chunks,))],
        compiler_params=params(),
        name="widen",
    )(landed)
    return (normed, residual_out, new_state, arrived)


def solution(mesh):
    return jax.shard_map(
        body,
        mesh=mesh,
        in_specs=(
            P("batch", None, None, "tensor"),
            P("batch", None, "tensor"),
            P("batch", "tensor", None, None),
            P(),
            P("tensor"),
            P("batch"),
            P("batch", None),
            P("batch", None),
            P("tensor"),
            P("tensor", None),
        ),
        out_specs=(
            P("batch", None, "tensor"),
            P("batch", None, "tensor"),
            P("batch", "tensor", None, None),
            P("batch", "tensor", None, None),
        ),
        check_vma=False,
    )
```
